256 devices in a mesh: cuts: 32 (over z, x_hi, core), band: 8 (over x_lo, y).
Axes of the slice: x: 4 (x_hi: 2, x_lo: 2; x = x_hi * 2 + x_lo), y: 4, z: 8, core: 2. Of those that a mesh axis runs over, the one named last changes fastest.
Arguments:
- eigvecs: bfloat16 [6144, 114688], P('band', 'cuts'), may hold values from -0.3984375 to 0.3984375
- energies: float32 [114688], P('cuts'), may hold values from -1 to 1
- smearing: float32 [114688], P('cuts'), may hold values from 0.05 to 1
- counts: int32 [64], P('cuts'), may hold values from 298 to 1792, as said below
- occupied: int32 [64], P('cuts'), may hold values from 1 to 1568, as said below
- block_cols: int32 [48, 3], P('band'), may hold values from 0 to 47, as said below
Outputs:
- density: float32 [6144, 384], P(('band', 'cuts'))
- energy_density: float32 [6144, 384], P(('band', 'cuts'))
The draws below stay inside these ranges and needn't reach their ends.
Inputs may be any that keep to these rules, and one draw needn't show every extreme that they name: `counts`: each slice has between 298 and 1792 eigenvectors; some slice has exactly 1792, some exactly 298. `occupied`: at least one and at most the slice's count, and at most 1568; both ends are reached. `block_cols`: row I holds I first, then two distinct block indices other than I that lie within 2 of I.
All inputs are finite; a program needn't handle non-finite values.
Results may differ from the reference program's by a relative error of at most 0.0029.
Values may be sent and summed in bfloat16 or wider, within the bound.
A program may use at most 128 MiB of HBM per device.

```python
import math
import jax
import jax.numpy as jnp
from jax import lax

BS = 128
COLS = 1792
NNZ = 3
SLICES = 64
NR = 6144
NBLK = 48


def shared_counts(key):
    first, second, third = jax.random.split(key, 3)
    lowest = COLS // 6
    base = jax.random.randint(first, (SLICES,), lowest, COLS + 1)
    fullest = jax.random.randint(second, (), 0, SLICES)
    thinnest = (fullest + 1) % SLICES
    place = jnp.arange(SLICES)
    filled = jnp.where(place == fullest, COLS, base)
    filled = jnp.where(place == thinnest, lowest, filled)
    eighths = jax.random.randint(third, (SLICES,), 1, 8)
    eighths = jnp.where(place == fullest, 7, eighths)
    occ = jnp.maximum(filled * eighths // 8, 1)
    occ = jnp.where(place == thinnest, 1, occ)
    return (filled.astype(jnp.int32), occ.astype(jnp.int32))


def draw_counts(key, part):
    return shared_counts(key)[0]


def draw_occupied(key, part):
    return shared_counts(key)[1]


def draw_block_cols(key, part):
    key = jax.random.fold_in(key, 7)
    blocks = jnp.arange(NBLK, dtype=jnp.int32)[:, None]
    offsets = jnp.array([-2, -1, 1, 2], dtype=jnp.int32)[None, :]
    target = blocks + offsets
    valid = (target >= 0) & (target < NBLK)
    scores = jax.random.randint(key, (NBLK, 4), 0, 1024) * 4 + jnp.arange(4, dtype=jnp.int32)[None, :]
    scores = jnp.where(valid, scores + 100000, scores)
    unused, picks = lax.top_k(scores, 2)
    chosen = jnp.take_along_axis(target, picks, axis=1)
    return jnp.concatenate([blocks, chosen], axis=1).astype(jnp.int32)


def with_spikes(entries, rng, source, target, blocks, factor):
    def block_of(axis_at):
        return (jnp.arange(entries.shape[axis_at]) // (entries.shape[axis_at] // blocks)).reshape((-1,) + (1,) * (entries.ndim - 1 - axis_at))

    one_side = jax.random.permutation(rng, blocks)[block_of(target)]
    other_side = (block_of(target) + blocks // 2) % blocks
    return jnp.where((block_of(source) == one_side) | (block_of(source) == other_side), factor * entries, entries)


def level_of(stream_key, extent, shards, smallest, high):
    def one(dim, shards_of):
        heights = jax.random.uniform(jax.random.fold_in(jax.random.fold_in(stream_key, 6), dim), (shards_of,), jnp.float32, smallest / len(shards), high / len(shards))
        return jnp.repeat(jnp.exp(heights), extent[dim] // shards_of).reshape((-1,) + (1,) * (len(extent) - dim - 1))

    factor_of = one(*shards[0])
    for cut in shards[1:]:
        factor_of = factor_of * one(*cut)
    return factor_of


def gaussian_with(rng, extent, scale, reach, pieces, heavy, kind=jnp.bfloat16):
    values = scale * jax.random.normal(rng, extent, jnp.float32)
    if pieces:
        values = values * level_of(rng, extent, pieces, -0.22, 0.18)
    return jnp.clip(with_spikes(values, jax.random.fold_in(rng, 3), *heavy), -reach, reach).astype(kind)


def setup_inputs(seed: int = 0) -> dict:
    key_list = jax.random.split(jax.random.key(seed), 7)
    return {
        "eigvecs": gaussian_with(key_list[0], (NR, SLICES * COLS), 0.06, 0.3984375, ((0, 8), (1, 32)), (1, 0, 32, 2.75)),
        "energies": jnp.clip(jax.random.uniform(key_list[1], (SLICES * COLS,), jnp.float32, -1.0, 1.0) * level_of(key_list[1], (SLICES * COLS,), ((0, 32),), -0.4, 0.0), -1.0, 1.0),
        "smearing": jnp.clip(jnp.exp(math.log(1.0) - 2.9957323 * jax.random.uniform(key_list[2], (SLICES * COLS,), jnp.float32) ** level_of(key_list[2], (SLICES * COLS,), ((0, 32),), -0.2, 0.2)), 0.05, 1.0),
        "counts": draw_counts(jax.random.fold_in(key_list[6], 71), 0),
        "occupied": draw_occupied(jax.random.fold_in(key_list[6], 71), 0),
        "block_cols": draw_block_cols(jax.random.fold_in(key_list[6], 71), 0),
    }


def reference(eigvecs, energies, smearing, counts, occupied, block_cols):
    slot = jnp.arange(COLS, dtype=jnp.int32)
    smear_rows = smearing.reshape(SLICES, COLS)
    energy_rows = energies.reshape(SLICES, COLS)
    live = slot[None, :] < counts[:, None]
    filled = slot[None, :] < occupied[:, None]
    weight = jnp.where(live, jnp.where(filled, jnp.float32(2.0), smear_rows), jnp.float32(0.0))
    weight_energy = weight * energy_rows
    row_index = (block_cols[:, :, None] * BS + jnp.arange(BS, dtype=jnp.int32)[None, None, :]).astype(jnp.int32)
    eig_three = eigvecs.reshape(NR, SLICES, COLS)

    def one_slice(carry, inputs):
        w_row, we_row, sidx = inputs
        part = lax.dynamic_index_in_dim(eig_three, sidx, 1, False)
        scaled = (part.astype(jnp.float32) * w_row[None, :]).astype(jnp.bfloat16)
        scaled_e = (part.astype(jnp.float32) * we_row[None, :]).astype(jnp.bfloat16)
        picked = scaled[row_index].astype(jnp.float32)
        picked_e = scaled_e[row_index].astype(jnp.float32)
        own = part.reshape(NBLK, BS, COLS).astype(jnp.float32)
        dens = jnp.einsum('bik,bjck->bijc', own, picked, precision=lax.Precision.HIGHEST)
        edens = jnp.einsum('bik,bjck->bijc', own, picked_e, precision=lax.Precision.HIGHEST)
        return (carry[0] + dens, carry[1] + edens), None

    zeros = jnp.zeros((NBLK, BS, NNZ, BS), jnp.float32)
    (dens, edens), unused = lax.scan(one_slice, (zeros, zeros), (weight, weight_energy, jnp.arange(SLICES, dtype=jnp.int32)))
    return dens.reshape(NR, NNZ * BS), edens.reshape(NR, NNZ * BS)
```

```python
import functools

import jax
import jax.numpy as jnp
from jax import lax
from jax.experimental import pallas as pl
from jax.experimental.pallas import tpu as pltpu
from jax.sharding import PartitionSpec as P

BS = 128
COLS = 1792
CHUNK = 512
MESH = pl.DeviceIdType.MESH
F32, BF16 = jnp.float32, jnp.bfloat16


def dot_t(a, b):
    return lax.dot_general(a, b, (((1,), (1,)), ((), ())), preferred_element_type=F32)


def kernel(
    nband, nz, cols_per_slice, chunk,
    eig, energies, smearing, counts, occupied, block_cols, dens, edens,
    e, halo, w, we, q, cross_a, cross_b,
    stage, pair_in, zsend, zrecv, xsum, xrecv,
    lstage, lpair_in, lsend, larecv, lbrecv, lxsum, lxrecv, late,
    load_sem, halo_ss, halo_rs, pair_ss, pair_rs, z_ss, z_rs, x_ss, x_rs,
    lpair_ss, lpair_rs, la_ss, la_rs, lb_ss, lb_rs, lx_ss, lx_rs,
):
    rows, cols = eig.shape
    nk = cols // chunk
    nblk = rows // BS
    own = dens.shape[0]
    rz = rows // nz
    low = -(-2 * BS // rz)
    high = nz - (rows - 2 * BS) // rz
    blow = -(-BS // rz)
    bhigh = nz - (rows - BS) // rz
    a_z = list(range(low)) + list(range(nz - high, nz))
    na = len(a_z)
    up_z = list(range(blow))
    dn_z = list(range(nz - bhigh, nz))

    me = lax.axis_index("cuts")
    band = lax.axis_index("band")
    z, xh, core = me // 4, me // 2 % 2, me % 2
    nxt, prv = (band + 1) % nband, (band + nband - 1) % nband
    lane = xh * 2 + core

    def dev(b, zz, x=None, c=None):
        return {"cuts": zz * 4 + (xh if x is None else x) * 2 + (core if c is None else c), "band": b}

    barrier = pltpu.get_barrier_semaphore()

    def greet(device):
        pl.semaphore_signal(barrier, inc=1, device_id=device, device_id_type=MESH)

    greet(dev(nxt, z))
    greet(dev(prv, z))
    greet(dev(band, z, c=1 - core))
    greet(dev(band, z, x=1 - xh))
    for k in range(1, nz):
        greet(dev(band, (z + k) % nz))

    @pl.when(z < blow)
    def _():
        for k in range(nz):
            greet(dev(prv, k))

    @pl.when(z >= nz - bhigh)
    def _():
        for k in range(nz):
            greet(dev(nxt, k))

    loads = []
    for k in range(nk):
        load = pltpu.make_async_copy(eig.at[:, pl.ds(k * chunk, chunk)], e.at[k], load_sem.at[k])
        load.start()
        loads.append(load)

    pl.semaphore_wait(barrier, 4 + (nz - 1) + blow + bhigh)

    def halo_copy(side, k):
        first = 0 if side == 0 else rows - BS
        start = k * chunk if isinstance(k, int) else pl.multiple_of(k * chunk, 128)
        return pltpu.make_async_remote_copy(
            src_ref=eig.at[pl.ds(first, BS), pl.ds(start, chunk)],
            dst_ref=halo.at[side, k],
            send_sem=halo_ss.at[side, k],
            recv_sem=halo_rs.at[side, k],
            device_id=dev(prv if side == 0 else nxt, z),
            device_id_type=MESH,
        )

    for k in range(nk):
        halo_copy(0, k).start()
        halo_copy(1, k).start()

    slot = lax.broadcasted_iota(jnp.int32, (1, cols), 1)
    weight = jnp.zeros((1, cols), F32)
    for s in range(cols // cols_per_slice):
        within = slot - s * cols_per_slice
        live = (within >= 0) & (within < counts[s])
        weight = jnp.where(live, jnp.where(within < occupied[s], 2.0, smearing[...]), weight)
    w[...] = weight
    we[...] = weight * energies[...]

    def scaled(block, k):
        at = pl.ds(pl.multiple_of(k * chunk, 128), chunk)
        wide = block.astype(F32)
        return jnp.concatenate(
            [(wide * w[:, at]).astype(BF16), (wide * we[:, at]).astype(BF16)], axis=0
        )

    q[...] = jnp.zeros_like(q)
    cross_a[...] = jnp.zeros_like(cross_a)
    cross_b[...] = jnp.zeros_like(cross_b)
    lstage[...] = jnp.zeros_like(lstage)
    late[...] = jnp.zeros_like(late)

    def inner(k, carry):
        pltpu.make_async_copy(
            eig.at[:, pl.ds(pl.multiple_of(k * chunk, 128), chunk)], e.at[k], load_sem.at[k]
        ).wait()
        for j in range(nblk):
            lo, hi = max(j - 2, 0), min(j + 3, nblk)
            got = dot_t(e[k, lo * BS : hi * BS, :], scaled(e[k, j * BS : (j + 1) * BS, :], k))
            for i in range(lo, hi):
                q[i * 5 + j - i + 2] += got[(i - lo) * BS : (i - lo + 1) * BS]
        return carry

    lax.fori_loop(0, nk, inner, 0)

    def place(target, block, row0, lanes):
        for o in range(row0 // own, -(-(row0 + BS) // own)):
            lo, hi = max(row0, own * o), min(row0 + BS, own * (o + 1))
            part = block[lo - row0 : hi - row0]
            at = (o % 2, o // 4, o // 2 % 2)
            target[at + (slice(lo - own * o, hi - own * o), lanes)] = part[:, :BS]
            target[at + (slice(own + lo - own * o, own + hi - own * o), lanes)] = part[:, BS:]

    first_block = band * nblk
    for i in range(nblk):
        for j in range(3):
            d = 2 if j == 0 else jnp.clip(block_cols[i, j] - first_block - i + 2, 0, 4)
            place(stage, q[i * 5 + d], i * BS, slice(j * BS, (j + 1) * BS))

    pair = pltpu.make_async_remote_copy(
        src_ref=stage.at[1 - core], dst_ref=pair_in, send_sem=pair_ss, recv_sem=pair_rs,
        device_id=dev(band, z, c=1 - core), device_id_type=MESH,
    )
    pair.start()

    def outer(k, carry):
        halo_copy(0, k).wait_recv()
        halo_copy(1, k).wait_recv()
        ahead, behind = halo[0, k], halo[1, k]
        cross_a[0] += dot_t(e[k, rows - 2 * BS :, :], scaled(ahead, k))
        cross_b[0] += dot_t(ahead, scaled(e[k, rows - 2 * BS : rows - BS, :], k))
        cross_a[1] += dot_t(e[k, : 2 * BS, :], scaled(behind, k))
        cross_b[1] += dot_t(behind, scaled(e[k, BS : 2 * BS, :], k))
        return carry

    first_cut, second_cut = max(nk * 2 // 7, 1), max(nk * 6 // 7, 1)
    lax.fori_loop(0, first_cut, outer, 0)

    pair.wait_recv()
    for t in range(nz):
        zsend[t] = (stage[core, t] + pair_in[t]).astype(BF16)

    def z_copy(k):
        there = (z + k) % nz
        return pltpu.make_async_remote_copy(
            src_ref=zsend.at[there], dst_ref=zrecv.at[k], send_sem=z_ss.at[k], recv_sem=z_rs.at[k],
            device_id=dev(band, there), device_id_type=MESH,
        )

    for k in range(1, nz):
        z_copy(k).start()

    lax.fori_loop(first_cut, second_cut, outer, 0)

    total = stage[core, z] + pair_in[z]
    for k in range(1, nz):
        z_copy(k).wait_recv()
        total = total + zrecv[k].astype(F32)
    xsum[...] = total
    x_copy = pltpu.make_async_remote_copy(
        src_ref=xsum.at[1 - xh], dst_ref=xrecv, send_sem=x_ss, recv_sem=x_rs,
        device_id=dev(band, z, x=1 - xh), device_id_type=MESH,
    )
    x_copy.start()

    lax.fori_loop(second_cut, nk, outer, 0)

    for s, zz in enumerate(a_z):
        for o in range(4 * zz, 4 * zz + 4):
            for side, base in ((1, 0), (0, rows - 2 * BS)):
                lo, hi = max(base, own * o), min(base + 2 * BS, own * (o + 1))
                if lo < hi:
                    at = (o % 2, s, o // 2 % 2)
                    lstage[at + (slice(lo - own * o, hi - own * o),)] = cross_a[side, lo - base : hi - base, :BS]
                    lstage[at + (slice(own + lo - own * o, own + hi - own * o),)] = cross_a[side, lo - base : hi - base, BS:]
    for s, (zz, side, base) in enumerate([(t, 0, 0) for t in up_z] + [(t, 1, rows - BS) for t in dn_z]):
        for o in range(4 * zz, 4 * zz + 4):
            lo, hi = max(base, own * o), min(base + BS, own * (o + 1))
            if lo < hi:
                at = (o % 2, na + s, o // 2 % 2)
                lstage[at + (slice(lo - own * o, hi - own * o),)] = cross_b[side, lo - base : hi - base, :BS]
                lstage[at + (slice(own + lo - own * o, own + hi - own * o),)] = cross_b[side, lo - base : hi - base, BS:]

    lpair = pltpu.make_async_remote_copy(
        src_ref=lstage.at[1 - core], dst_ref=lpair_in, send_sem=lpair_ss, recv_sem=lpair_rs,
        device_id=dev(band, z, c=1 - core), device_id_type=MESH,
    )
    lpair.start()
    lpair.wait_recv()
    lsend[...] = (lstage[core] + lpair_in[...]).astype(BF16)

    def a_copy(s, zz, origin):
        return pltpu.make_async_remote_copy(
            src_ref=lsend.at[s], dst_ref=larecv.at[origin], send_sem=la_ss.at[s], recv_sem=la_rs.at[origin],
            device_id=dev(band, zz), device_id_type=MESH,
        )

    def b_copy(s, b, zz, origin):
        return pltpu.make_async_remote_copy(
            src_ref=lsend.at[na + s], dst_ref=lbrecv.at[origin], send_sem=lb_ss.at[s], recv_sem=lb_rs.at[origin],
            device_id=dev(b, zz), device_id_type=MESH,
        )

    b_list = [(s, nxt, zz) for s, zz in enumerate(up_z)]
    b_list += [(blow + s, prv, zz) for s, zz in enumerate(dn_z)]
    for s, b, zz in b_list:
        b_copy(s, b, zz, z).start()
    for s, zz in enumerate(a_z):
        pl.when(z != zz)(a_copy(s, zz, z).start)

    is_a = (z < low) | (z >= nz - high)
    is_b = (z < blow) | (z >= nz - bhigh)

    lx = pltpu.make_async_remote_copy(
        src_ref=lxsum.at[1 - xh], dst_ref=lxrecv, send_sem=lx_ss, recv_sem=lx_rs,
        device_id=dev(band, z, x=1 - xh), device_id_type=MESH,
    )

    @pl.when(is_a)
    def _():
        mine = jnp.where(z < low, z, z - (nz - na))
        sum_a = lstage[core, mine] + lpair_in[mine]
        for k in range(1, nz):
            origin = (z + k) % nz
            a_copy(0, 0, origin).wait_recv()
            sum_a = sum_a + larecv[origin].astype(F32)
        lxsum[:, 0] = sum_a
        lxsum[:, 1] = jnp.zeros_like(sum_a)

        @pl.when(is_b)
        def _():
            sum_b = jnp.zeros_like(sum_a)
            for k in range(nz):
                b_copy(0, nxt, 0, k).wait_recv()
                sum_b = sum_b + lbrecv[k].astype(F32)
            lxsum[:, 1] = sum_b

        lx.start()
        lx.wait_recv()
        late[...] = lxsum[xh] + lxrecv[...]

    x_copy.wait_recv()
    early = xsum[xh] + xrecv[...]
    row_block = (lax.broadcasted_iota(jnp.int32, (own, BS), 0) + own * me) // BS
    for j in range(3):
        for out, start in ((dens, 0), (edens, own)):
            value = early[start : start + own, j * BS : (j + 1) * BS]
            if j:
                for part, wanted in (
                    (0, ((0, -1), (1, -1), (nblk - 2, nblk), (nblk - 1, nblk))),
                    (1, ((0, -2), (nblk - 1, nblk + 1))),
                ):
                    mask = None
                    for i, rel in wanted:
                        hit = jnp.where(block_cols[i, j] - first_block == rel, i, -1)
                        mask = (row_block == hit) if mask is None else mask | (row_block == hit)
                    value = value + jnp.where(mask, late[part, start : start + own, :], 0.0)
            out[:, j * BS : (j + 1) * BS] = value

    for k in range(nk):
        halo_copy(0, k).wait_send()
        halo_copy(1, k).wait_send()
    pair.wait_send()
    for k in range(1, nz):
        z_copy(k).wait_send()
    x_copy.wait_send()
    lpair.wait_send()
    for s, b, zz in b_list:
        b_copy(s, b, zz, z).wait_send()
    for s, zz in enumerate(a_z):
        pl.when(z != zz)(a_copy(s, zz, z).wait_send)
    pl.when(is_a)(lx.wait_send)


def shards(nband, nz, cols_per_slice, chunk, eigvecs, energies, smearing, counts, occupied, block_cols):
    rows, cols = eigvecs.shape
    nk = cols // chunk
    nblk = rows // BS
    own = rows // (nz * 4)
    rz = rows // nz
    na = -(-2 * BS // rz) + nz - (rows - 2 * BS) // rz
    nb = -(-BS // rz) + nz - (rows - BS) // rz
    vmem = pl.BlockSpec(memory_space=pltpu.VMEM)
    smem = pl.BlockSpec(memory_space=pltpu.SMEM)
    dma = pltpu.SemaphoreType.DMA
    wide = 3 * BS
    return pl.pallas_call(
        functools.partial(kernel, nband, nz, cols_per_slice, chunk),
        out_shape=(jax.ShapeDtypeStruct((own, wide), F32),) * 2,
        in_specs=[pl.BlockSpec(memory_space=pl.ANY), vmem, vmem, smem, smem, smem],
        out_specs=(vmem, vmem),
        scratch_shapes=[
            pltpu.VMEM((nk, rows, chunk), BF16),
            pltpu.VMEM((2, nk, BS, chunk), BF16),
            pltpu.VMEM((1, cols), F32),
            pltpu.VMEM((1, cols), F32),
            pltpu.VMEM((nblk * 5, BS, 2 * BS), F32),
            pltpu.VMEM((2, 2 * BS, 2 * BS), F32),
            pltpu.VMEM((2, BS, 2 * BS), F32),
            pltpu.VMEM((2, nz, 2, 2 * own, wide), F32),
            pltpu.VMEM((nz, 2, 2 * own, wide), F32),
            pltpu.VMEM((nz, 2, 2 * own, wide), BF16),
            pltpu.VMEM((nz, 2, 2 * own, wide), BF16),
            pltpu.VMEM((2, 2 * own, wide), F32),
            pltpu.VMEM((2 * own, wide), F32),
            pltpu.VMEM((2, na + nb, 2, 2 * own, BS), F32),
            pltpu.VMEM((na + nb, 2, 2 * own, BS), F32),
            pltpu.VMEM((na + nb, 2, 2 * own, BS), BF16),
            pltpu.VMEM((nz, 2, 2 * own, BS), BF16),
            pltpu.VMEM((nz, 2, 2 * own, BS), BF16),
            pltpu.VMEM((2, 2, 2 * own, BS), F32),
            pltpu.VMEM((2, 2 * own, BS), F32),
            pltpu.VMEM((2, 2 * own, BS), F32),
            dma((nk,)), dma((2, nk)), dma((2, nk)), dma, dma, dma((nz,)), dma((nz,)), dma, dma,
            dma, dma, dma((na,)), dma((nz,)), dma((nb,)), dma((nz,)), dma, dma,
        ],
        compiler_params=pltpu.CompilerParams(
            collective_id=0, has_side_effects=True, vmem_limit_bytes=48 * 1024 * 1024
        ),
        cost_estimate=pl.CostEstimate(
            flops=2 * 48 * BS * BS * cols, bytes_accessed=rows * cols * 2, transcendentals=0
        ),
    )(eigvecs, energies.reshape(1, cols), smearing.reshape(1, cols), counts, occupied, block_cols)


def build(mesh, cols_per_slice, chunk):
    placed = (P("band", "cuts"), P("cuts"), P("cuts"), P("cuts"), P("cuts"), P("band", None))
    body = functools.partial(shards, mesh.shape["band"], mesh.shape["cuts"] // 4, cols_per_slice, chunk)
    return jax.shard_map(
        body,
        mesh=mesh,
        in_specs=placed,
        out_specs=(P(("band", "cuts"), None), P(("band", "cuts"), None)),
        check_vma=False,
    )


def solution(mesh):
    return build(mesh, COLS, CHUNK)
```

```python
import functools

import jax
import jax.numpy as jnp
from jax import lax
from jax.experimental import pallas as pl
from jax.experimental.pallas import tpu as pltpu
from jax.sharding import PartitionSpec as P

BS = 128
COLS = 1792
CHUNK = 512
HALF = BS // 2
VMEM_LIMIT = 60 * 1024 * 1024
MESH = pl.DeviceIdType.MESH
F32, BF16 = jnp.float32, jnp.bfloat16


def dot_t(a, b):
    return lax.dot_general(a, b, (((1,), (1,)), ((), ())), preferred_element_type=F32)


def kernel(
    nband, nz, cols_per_slice, chunk,
    eig, energies_in, smearing_in, counts_in, occupied_in, cols_in, dens, edens,
    energies, smearing, counts, occupied, block_cols, e, halo, w, we, sb, q, cross_a, cross_b,
    stage, pair_in, rsend, rrecv, xsum, xrecv,
    lstage, lpair_in, lsend, larecv, lbrecv, lxsum, lxrecv, late,
    small_sem, load_sem, halo_ss, halo_rs, pair_ss, pair_rs, r_ss, r_rs, x_ss, x_rs,
    lpair_ss, lpair_rs, la_ss, la_rs, lb_ss, lb_rs, lx_ss, lx_rs,
):
    rows, cols = eig.shape
    nk = cols // chunk
    nblk = rows // BS
    own = dens.shape[0]
    rz = rows // nz
    steps = nz // 2
    a_z = outer_z(rows, nz)
    na = len(a_z)
    low = na // 2
    b_z = [boundary_z(rows, nz, p) for p in range(2)]
    up_all = sorted(set(b_z[0][0] + b_z[1][0]))
    dn_all = sorted(set(b_z[0][1] + b_z[1][1]))

    me = lax.axis_index("cuts")
    band = lax.axis_index("band")
    z, xh, core = me // 4, me // 2 % 2, me % 2
    nxt, prv = (band + 1) % nband, (band + nband - 1) % nband

    def dev(b, zz, x=None, c=None):
        return {"cuts": zz * 4 + (xh if x is None else x) * 2 + (core if c is None else c), "band": b}

    def remote(src, dst, send_sem, recv_sem, device):
        return pltpu.make_async_remote_copy(
            src_ref=src, dst_ref=dst, send_sem=send_sem, recv_sem=recv_sem,
            device_id=device, device_id_type=MESH,
        )

    barrier = pltpu.get_barrier_semaphore()

    def greet(device):
        pl.semaphore_signal(barrier, inc=1, device_id=device, device_id_type=MESH)

    greet(dev(nxt, z))
    greet(dev(prv, z))
    greet(dev(band, z, c=1 - core))
    greet(dev(band, z, x=1 - xh))
    for k in range(1, nz):
        greet(dev(band, (z + k) % nz))

    @pl.when(z < len(up_all))
    def _():
        for k in range(nz):
            greet(dev(prv, k))

    @pl.when(z >= nz - len(dn_all))
    def _():
        for k in range(nz):
            greet(dev(nxt, k))

    smalls = []
    for t, (src, dst) in enumerate((
        (energies_in, energies), (smearing_in, smearing),
        (counts_in, counts), (occupied_in, occupied), (cols_in, block_cols),
    )):
        small = pltpu.make_async_copy(src, dst, small_sem.at[t])
        small.start()
        smalls.append(small)
    for k in range(nk):
        pltpu.make_async_copy(eig.at[:, pl.ds(k * chunk, chunk)], e.at[k], load_sem.at[k]).start()

    pl.semaphore_wait(barrier, 4 + (nz - 1) + len(up_all) + len(dn_all))

    def halo_copy(p, side, k):
        first = HALF * (1 - p) if side == 0 else rows - BS + HALF * p
        start = k * chunk if isinstance(k, int) else pl.multiple_of(k * chunk, 128)
        return remote(
            eig.at[pl.ds(first, HALF), pl.ds(start, chunk)], halo.at[p, side, k],
            halo_ss.at[p, side, k], halo_rs.at[p, side, k], dev(prv if side == 0 else nxt, z),
        )

    for p in range(2):
        for k in range(nk):
            halo_copy(p, 0, k).start()
            halo_copy(p, 1, k).start()

    for small in smalls:
        small.wait()
    slot = lax.broadcasted_iota(jnp.int32, (1, cols), 1)
    weight = jnp.zeros((1, cols), F32)
    for s in range(cols // cols_per_slice):
        within = slot - s * cols_per_slice
        live = (within >= 0) & (within < counts[s])
        weight = jnp.where(live, jnp.where(within < occupied[s], 2.0, smearing[...].reshape(1, cols)), weight)
    w[...] = weight
    we[...] = weight * energies[...].reshape(1, cols)

    def scaled(block, k):
        at = pl.ds(pl.multiple_of(k * chunk, 128), chunk)
        wide = block.astype(F32)
        return jnp.concatenate(
            [(wide * w[:, at]).astype(BF16), (wide * we[:, at]).astype(BF16)], axis=0
        )

    q[...] = jnp.zeros_like(q)
    cross_a[...] = jnp.zeros_like(cross_a)
    cross_b[...] = jnp.zeros_like(cross_b)
    lstage[...] = jnp.zeros_like(lstage)
    late[...] = jnp.zeros_like(late)
    lxsum[...] = jnp.zeros_like(lxsum)

    def inner(k, carry):
        pltpu.make_async_copy(
            eig.at[:, pl.ds(pl.multiple_of(k * chunk, 128), chunk)], e.at[k], load_sem.at[k]
        ).wait()
        for j in range(nblk):
            lo, hi = max(j - 2, 0), min(j + 3, nblk)
            both = scaled(e[k, j * BS : (j + 1) * BS, :], k)
            if j == nblk - 2:
                sb[0, k] = both
            if j == 1:
                sb[1, k] = both
            got = dot_t(e[k, lo * BS : hi * BS, :], both)
            for i in range(lo, hi):
                q[i * 5 + j - i + 2] += got[(i - lo) * BS : (i - lo + 1) * BS]
        return carry

    lax.fori_loop(0, nk, inner, 0)

    first_block = band * nblk
    for i in range(nblk):
        for j in range(3):
            d = 2 if j == 0 else jnp.clip(block_cols[j, i] - first_block - i + 2, 0, 4)
            block = q[i * 5 + d]
            lanes = slice(j * BS, (j + 1) * BS)
            for o in range(i * BS // own, -(-(i + 1) * BS // own)):
                lo, hi = max(i * BS, own * o), min((i + 1) * BS, own * (o + 1))
                part = block[lo - i * BS : hi - i * BS]
                at = (o % 2, o // 4, o // 2 % 2)
                stage[at + (slice(lo - own * o, hi - own * o), lanes)] = part[:, :BS]
                stage[at + (slice(own + lo - own * o, own + hi - own * o), lanes)] = part[:, BS:]

    pair = remote(stage.at[1 - core], pair_in, pair_ss, pair_rs, dev(band, z, c=1 - core))
    pair.start()

    def outer(p, begin, end):
        def body(k, carry):
            halo_copy(p, 0, k).wait_recv()
            halo_copy(p, 1, k).wait_recv()
            ahead, behind = halo[p, 0, k], halo[p, 1, k]
            cross_a[p, 0] += dot_t(e[k, rows - 2 * BS :, :], scaled(ahead, k))
            cross_b[p, 0] += dot_t(ahead, sb[0, k])
            cross_a[p, 1] += dot_t(e[k, : 2 * BS, :], scaled(behind, k))
            cross_b[p, 1] += dot_t(behind, sb[1, k])
            return carry

        lax.fori_loop(begin, end, body, 0)

    def mine(zz):
        return stage[core, zz] + pair_in[zz]

    def ring_copy(d, t):
        at = (d, t, d) if t == 0 else (d, t)
        return remote(
            rsend.at[at], rrecv.at[at], r_ss.at[d, t], r_rs.at[d, t],
            dev(band, (z + (1 if d == 0 else nz - 1)) % nz),
        )

    def ring(t):
        for d in range(2):
            far = steps - t
            chunk_sum = mine((z + far) % nz if d == 0 else (z + nz - far) % nz)
            if t == 0:
                rsend[d, 0, d] = chunk_sum[d].astype(BF16)
            else:
                ring_copy(d, t - 1).wait_recv()
                if t == 1:
                    rsend[d, 1, 1 - d] = chunk_sum[1 - d].astype(BF16)
                    rsend[d, 1, d] = (chunk_sum[d] + rrecv[d, 0, d].astype(F32)).astype(BF16)
                else:
                    rsend[d, t] = (chunk_sum + rrecv[d, t - 1].astype(F32)).astype(BF16)
            ring_copy(d, t).start()

    def ring_end():
        total = mine(z)
        for d in range(2):
            ring_copy(d, steps - 1).wait_recv()
            if steps == 1:
                xsum[d] = total[d] + rrecv[d, 0, d].astype(F32)
            else:
                total = total + rrecv[d, steps - 1].astype(F32)
        if steps > 1:
            xsum[...] = total

    x_copy = remote(xsum.at[1 - xh], xrecv, x_ss, x_rs, dev(band, z, x=1 - xh))

    def late_pack(p):
        regions = [(s, zz, side, base, 2 * BS, None) for s, zz in enumerate(a_z)
                   for side, base in ((1, 0), (0, rows - 2 * BS))]
        up, dn = b_z[p]
        regions += [(na + 2 * s, zz, 0, HALF * (1 - p), HALF, 0) for s, zz in enumerate(up)]
        regions += [(na + 2 * (len(up) + s), zz, 1, rows - BS + HALF * p, HALF, 0) for s, zz in enumerate(dn)]
        for s, zz, side, base, length, two in regions:
            for o in range(4 * zz, 4 * zz + 4):
                lo, hi = max(base, own * o), min(base + length, own * (o + 1))
                if lo < hi:
                    to = slice(o // 2 % 2 * own + lo - own * o, o // 2 % 2 * own + hi - own * o)
                    if two is None:
                        lstage[p, o % 2, s, to] = cross_a[p, side, lo - base : hi - base]
                    else:
                        lstage[p, o % 2, s, to] = cross_b[p, side, lo - base : hi - base, :BS]
                        lstage[p, o % 2, s + 1, to] = cross_b[p, side, lo - base : hi - base, BS:]

    def late_pair(p):
        return remote(
            lstage.at[p, 1 - core], lpair_in.at[p], lpair_ss.at[p], lpair_rs.at[p],
            dev(band, z, c=1 - core),
        )

    def a_copy(p, s, zz, origin):
        return remote(
            lsend.at[p, s], larecv.at[p, origin], la_ss.at[p, s], la_rs.at[p, origin], dev(band, zz)
        )

    def b_copy(p, s, b, zz, origin):
        return remote(
            lsend.at[p, pl.ds(na + 2 * s, 2)], lbrecv.at[p, origin], lb_ss.at[p, s], lb_rs.at[p, origin],
            dev(b, zz),
        )

    def b_list(p):
        up, dn = b_z[p]
        return [(s, nxt, zz) for s, zz in enumerate(up)] + [
            (len(up) + s, prv, zz) for s, zz in enumerate(dn)
        ]

    def late_send(p):
        late_pair(p).wait_recv()
        lsend[p] = (lstage[p, core] + lpair_in[p]).astype(BF16)
        for s, b, zz in b_list(p):
            b_copy(p, s, b, zz, z).start()
        for s, zz in enumerate(a_z):
            pl.when(z != zz)(a_copy(p, s, zz, z).start)

    is_a = (z < low) | (z >= nz - low)
    is_b = [(z <= max(up)) | (z >= min(dn)) for up, dn in b_z]

    def late_x(p):
        return remote(
            lxsum.at[p, :, pl.ds(pl.multiple_of((1 - xh) * own, 8), own)], lxrecv.at[p],
            lx_ss.at[p], lx_rs.at[p], dev(band, z, x=1 - xh),
        )

    def late_sum(p):
        @pl.when(is_a)
        def _():
            at = jnp.where(z < low, z, z - (nz - na))
            sum_a = lstage[p, core, at] + lpair_in[p, at]
            for k in range(1, nz):
                origin = (z + k) % nz
                a_copy(p, 0, 0, origin).wait_recv()
                sum_a = sum_a + larecv[p, origin].astype(F32)
            lxsum[p, 0] = sum_a

            @pl.when(is_b[p])
            def _():
                sum_b = jnp.zeros(lxsum.shape[2:], F32)[None]
                for k in range(nz):
                    b_copy(p, 0, nxt, 0, k).wait_recv()
                    sum_b = sum_b + lbrecv[p, k].astype(F32)
                lxsum[p, 1:] = sum_b

            late_x(p).start()

    def late_end(p):
        @pl.when(is_a)
        def _():
            late_x(p).wait_recv()
            late[p] = lxsum[p, :, pl.ds(pl.multiple_of(xh * own, 8), own)] + lxrecv[p]

    def cut(part):
        return nk * part // 7

    outer(0, 0, nk)
    pair.wait_recv()
    ring(0)
    late_pack(0)
    late_pair(0).start()
    for t in range(1, steps):
        ring(t)
        outer(1, cut(2 * t - 2), cut(2 * t))
        if t == 1:
            late_send(0)
    if steps == 1:
        late_send(0)
    late_sum(0)
    outer(1, cut(2 * steps - 2), nk)
    late_pack(1)
    late_pair(1).start()
    ring_end()
    x_copy.start()
    late_send(1)
    late_end(0)
    x_copy.wait_recv()
    early = xsum[xh] + xrecv[...]
    late_sum(1)
    late_end(1)

    row_block = (lax.broadcasted_iota(jnp.int32, (own, BS), 0) + own * me) // BS
    top = z < steps
    near = jnp.where(top, late[0, 0], late[1, 0])
    far = jnp.where(top, late[1, 0], late[0, 0])
    for out, start, lanes, row in ((dens, 0, slice(0, HALF), 1), (edens, own, slice(HALF, BS), 2)):
        parts = (
            jnp.concatenate([near[:, lanes], far[:, lanes]], axis=1),
            late[0, row] + late[1, row],
        )
        for j in range(3):
            value = early[start : start + own, j * BS : (j + 1) * BS]
            if j:
                for part, wanted in (
                    (parts[0], ((0, -1), (1, -1), (nblk - 2, nblk), (nblk - 1, nblk))),
                    (parts[1], ((0, -2), (nblk - 1, nblk + 1))),
                ):
                    mask = None
                    for i, rel in wanted:
                        hit = jnp.where(block_cols[j, i] - first_block == rel, i, -1)
                        mask = (row_block == hit) if mask is None else mask | (row_block == hit)
                    value = value + jnp.where(mask, part, 0.0)
            out[:, j * BS : (j + 1) * BS] = value

    pair.wait_send()
    x_copy.wait_send()
    for t in range(steps):
        for d in range(2):
            ring_copy(d, t).wait_send()
    for p in range(2):
        for k in range(nk):
            halo_copy(p, 0, k).wait_send()
            halo_copy(p, 1, k).wait_send()
        late_pair(p).wait_send()
        for s, b, zz in b_list(p):
            b_copy(p, s, b, zz, z).wait_send()
        for s, zz in enumerate(a_z):
            pl.when(z != zz)(a_copy(p, s, zz, z).wait_send)
        pl.when(is_a)(late_x(p).wait_send)


def outer_z(rows, nz):
    rz = rows // nz
    low = -(-2 * BS // rz)
    return list(range(low)) + list(range(nz - low, nz))


def boundary_z(rows, nz, p):
    rz = rows // nz
    base = HALF * (1 - p)
    up = list(range(base // rz, -(-(base + HALF) // rz)))
    base = rows - BS + HALF * p
    return up, list(range(base // rz, -(-(base + HALF) // rz)))


def shards(nband, nz, cols_per_slice, chunk, eigvecs, energies, smearing, counts, occupied, block_cols):
    rows, cols = eigvecs.shape
    nk = cols // chunk
    nblk = rows // BS
    own = rows // (nz * 4)
    na = len(outer_z(rows, nz))
    nb = max(len(up) + len(dn) for up, dn in (boundary_z(rows, nz, p) for p in range(2)))
    nl = na + 2 * nb
    steps = nz // 2
    vmem = pl.BlockSpec(memory_space=pltpu.VMEM)
    dma = pltpu.SemaphoreType.DMA
    wide = 3 * BS
    return pl.pallas_call(
        functools.partial(kernel, nband, nz, cols_per_slice, chunk),
        out_shape=(jax.ShapeDtypeStruct((own, wide), F32),) * 2,
        in_specs=[pl.BlockSpec(memory_space=pl.ANY)] * 6,
        out_specs=(vmem, vmem),
        scratch_shapes=[
            pltpu.VMEM((cols,), F32),
            pltpu.VMEM((cols,), F32),
            pltpu.SMEM(counts.shape, jnp.int32),
            pltpu.SMEM(occupied.shape, jnp.int32),
            pltpu.SMEM((3, nblk), jnp.int32),
            pltpu.VMEM((nk, rows, chunk), BF16),
            pltpu.VMEM((2, 2, nk, HALF, chunk), BF16),
            pltpu.VMEM((1, cols), F32),
            pltpu.VMEM((1, cols), F32),
            pltpu.VMEM((2, nk, 2 * BS, chunk), BF16),
            pltpu.VMEM((nblk * 5, BS, 2 * BS), F32),
            pltpu.VMEM((2, 2, 2 * BS, BS), F32),
            pltpu.VMEM((2, 2, HALF, 2 * BS), F32),
            pltpu.VMEM((2, nz, 2, 2 * own, wide), F32),
            pltpu.VMEM((nz, 2, 2 * own, wide), F32),
            pltpu.VMEM((2, steps, 2, 2 * own, wide), BF16),
            pltpu.VMEM((2, steps, 2, 2 * own, wide), BF16),
            pltpu.VMEM((2, 2 * own, wide), F32),
            pltpu.VMEM((2 * own, wide), F32),
            pltpu.VMEM((2, 2, nl, 2 * own, BS), F32),
            pltpu.VMEM((2, nl, 2 * own, BS), F32),
            pltpu.VMEM((2, nl, 2 * own, BS), BF16),
            pltpu.VMEM((2, nz, 2 * own, BS), BF16),
            pltpu.VMEM((2, nz, 2, 2 * own, BS), BF16),
            pltpu.VMEM((2, 3, 2 * own, BS), F32),
            pltpu.VMEM((2, 3, own, BS), F32),
            pltpu.VMEM((2, 3, own, BS), F32),
            dma((5,)), dma((nk,)), dma((2, 2, nk)), dma((2, 2, nk)), dma, dma,
            dma((2, steps)), dma((2, steps)), dma, dma,
            dma((2,)), dma((2,)), dma((2, na)), dma((2, nz)), dma((2, nb)), dma((2, nz)), dma((2,)), dma((2,)),
        ],
        compiler_params=pltpu.CompilerParams(
            collective_id=0, has_side_effects=True, vmem_limit_bytes=VMEM_LIMIT
        ),
        cost_estimate=pl.CostEstimate(
            flops=2 * 48 * BS * BS * cols, bytes_accessed=rows * cols * 2, transcendentals=0
        ),
    )(eigvecs, energies, smearing, counts, occupied, block_cols.T)


def build(mesh, cols_per_slice, chunk):
    placed = (P("band", "cuts"), P("cuts"), P("cuts"), P("cuts"), P("cuts"), P("band", None))
    body = functools.partial(shards, mesh.shape["band"], mesh.shape["cuts"] // 4, cols_per_slice, chunk)
    return jax.shard_map(
        body,
        mesh=mesh,
        in_specs=placed,
        out_specs=(P(("band", "cuts"), None), P(("band", "cuts"), None)),
        check_vma=False,
    )


def solution(mesh):
    return build(mesh, COLS, CHUNK)
```

```python
import functools

import jax
import jax.numpy as jnp
from jax import lax
from jax.experimental import pallas as pl
from jax.experimental.pallas import tpu as pltpu
from jax.sharding import PartitionSpec as P

BS = 128
COLS = 1792
CHUNK = 512
SPLIT = ((0, 96), (96, 32))
VMEM_LIMIT = 60 * 1024 * 1024
MESH = pl.DeviceIdType.MESH
F32, BF16 = jnp.float32, jnp.bfloat16


def dot_t(a, b):
    return lax.dot_general(a, b, (((1,), (1,)), ((), ())), preferred_element_type=F32)


def kernel(
    nband, nz, cols_per_slice, chunk,
    eig, energies_in, smearing_in, counts_in, occupied_in, cols_in, dens, edens,
    energies, smearing, counts, occupied, block_cols, e, w, we, ss, q,
    halo0, halo1, cross_a0, cross_a1, cross_b0, cross_b1,
    stage0, stage1, pair0, pair1, rsend0, rsend1, rrecv0, rrecv1, xsum, xrecv,
    lstage0, lstage1, lpair0, lpair1, lsend0, lsend1, larecv0, larecv1, lbrecv0, lbrecv1,
    lxsum, lxrecv, late_a0, late_a1, late_b,
    wave, ready, small_sem, load_sem, halo_ss, halo_rs, pair_ss, pair_rs, r_ss, r_rs, x_ss, x_rs,
    lpair_ss, lpair_rs, la_ss, la_rs, lb_ss, lb_rs, lx_ss, lx_rs,
):
    rows, cols = eig.shape
    nk = cols // chunk
    nblk = rows // BS
    own = dens.shape[0]
    hr = packed_rows(own)
    ng = 2 * nz
    halo, cross_a, cross_b = (halo0, halo1), (cross_a0, cross_a1), (cross_b0, cross_b1)
    lstage, lpair_in, lsend = (lstage0, lstage1), (lpair0, lpair1), (lsend0, lsend1)
    larecv, lbrecv = (larecv0, larecv1), (lbrecv0, lbrecv1)
    stage, pair_in, rsend, rrecv = (stage0, stage1), (pair0, pair1), (rsend0, rsend1), (rrecv0, rrecv1)
    a_rows = (2 * own, hr)
    a_g = outer_groups(rows, nz)
    na = len(a_g)
    b_g = [boundary_groups(rows, nz, p) for p in range(2)]

    me = lax.axis_index("cuts")
    band = lax.axis_index("band")
    g, core = me // 2, me % 2
    z, xh = g // 2, g % 2
    nxt, prv = (band + 1) % nband, (band + nband - 1) % nband

    def dev(b, gg):
        return {"cuts": gg * 2 + core, "band": b}

    across = {"cuts": z * 4 + (1 - xh) * 2 + core, "band": band}
    partner = {"cuts": g * 2 + 1 - core, "band": band}

    def remote(src, dst, send_sem, recv_sem, device):
        return pltpu.make_async_remote_copy(
            src_ref=src, dst_ref=dst, send_sem=send_sem, recv_sem=recv_sem,
            device_id=device, device_id_type=MESH,
        )

    barrier = pltpu.get_barrier_semaphore()

    def greet(device):
        pl.semaphore_signal(barrier, inc=1, device_id=device, device_id_type=MESH)

    greet(dev(nxt, g))
    greet(dev(prv, g))
    ring = (dev(band, (z + 1) % nz * 2 + xh), dev(band, (z + nz - 1) % nz * 2 + xh))
    greet(ring[0])
    greet(ring[1])
    greet(across)
    greet(partner)

    smalls = []
    for t, (src, dst) in enumerate((
        (energies_in, energies), (smearing_in, smearing),
        (counts_in, counts), (occupied_in, occupied), (cols_in, block_cols),
    )):
        small = pltpu.make_async_copy(src, dst, small_sem.at[t])
        small.start()
        smalls.append(small)
    for k in range(nk):
        pltpu.make_async_copy(eig.at[:, pl.ds(k * chunk, chunk)], e.at[k], load_sem.at[k]).start()

    pl.semaphore_wait(barrier, 6)

    def halo_copy(p, side, k):
        q0, n = SPLIT[p]
        first = q0 if side == 0 else rows - BS + q0
        start = k * chunk if isinstance(k, int) else pl.multiple_of(k * chunk, 128)
        return remote(
            eig.at[pl.ds(first, n), pl.ds(start, chunk)], halo[p].at[side, k],
            halo_ss.at[p, side, k], halo_rs.at[p, side, k], dev(prv if side == 0 else nxt, g),
        )

    for p in range(2):
        for k in range(nk):
            halo_copy(p, 0, k).start()
            halo_copy(p, 1, k).start()

    def tell(sem, device):
        pl.semaphore_signal(sem, inc=1, device_id=device, device_id_type=MESH)

    def relay(t):
        for d in range(2):
            if t:
                pl.semaphore_wait(wave.at[d, t - 1], 1)
            if t < nz // 2:
                tell(wave.at[d, t], ring[d])
            elif d == 1:
                tell(ready.at[0], dev(nxt, g))
                tell(ready.at[1], dev(prv, g))

    relay(0)
    for small in smalls:
        small.wait()
    slot = lax.broadcasted_iota(jnp.int32, (1, cols), 1)
    weight = jnp.zeros((1, cols), F32)
    for s in range(cols // cols_per_slice):
        within = slot - s * cols_per_slice
        live = (within >= 0) & (within < counts[s])
        weight = jnp.where(live, jnp.where(within < occupied[s], 2.0, smearing[...].reshape(1, cols)), weight)
    w[...] = weight
    we[...] = weight * energies[...].reshape(1, cols)

    def scaled(block, k, pad=0):
        at = pl.ds(pl.multiple_of(k * chunk, 128), chunk)
        wide = block.astype(F32)
        parts = [(wide * w[:, at]).astype(BF16), (wide * we[:, at]).astype(BF16)]
        if pad:
            gap = jnp.zeros((pad, chunk), BF16)
            parts = [parts[0], gap, parts[1], gap]
        return jnp.concatenate(parts, axis=0)

    for ref in (q, cross_a0, cross_a1, cross_b0, cross_b1, lstage0, lstage1, lxsum, late_a0, late_a1, late_b):
        ref[...] = jnp.zeros_like(ref)

    def diagonal(k, carry):
        pltpu.make_async_copy(
            eig.at[:, pl.ds(pl.multiple_of(k * chunk, 128), chunk)], e.at[k], load_sem.at[k]
        ).wait()
        for j in range(nblk):
            block = e[k, j * BS : (j + 1) * BS, :]
            both = scaled(block, k)
            ss[j, k] = both
            q[j * 5 + 2] += dot_t(block, both)
        return carry

    def others(k, carry):
        for j in range(nblk):
            near = [i for i in range(max(j - 2, 0), min(j + 3, nblk)) if i != j]
            left = jnp.concatenate([e[k, i * BS : (i + 1) * BS, :] for i in near], axis=0)
            got = dot_t(left, ss[j, k])
            for t, i in enumerate(near):
                q[i * 5 + j - i + 2] += got[t * BS : (t + 1) * BS]
        return carry

    first_block = band * nblk

    def early_pack(h):
        for i in range(nblk):
            for j in ((0,), (1, 2))[h]:
                d = 2 if j == 0 else jnp.clip(block_cols[j, i] - first_block - i + 2, 0, 4)
                block = q[i * 5 + d]
                lanes = slice((j - h) * BS, (j - h + 1) * BS)
                for o in range(i * BS // own, -(-(i + 1) * BS // own)):
                    lo, hi = max(i * BS, own * o), min((i + 1) * BS, own * (o + 1))
                    part = block[lo - i * BS : hi - i * BS]
                    at = (o % 2, o // 2)
                    stage[h][at + (slice(lo - own * o, hi - own * o), lanes)] = part[:, :BS]
                    stage[h][at + (slice(own + lo - own * o, own + hi - own * o), lanes)] = part[:, BS:]

    def early_pair(h):
        return remote(stage[h].at[1 - core], pair_in[h], pair_ss.at[h], pair_rs.at[h], partner)

    hops = nz // 2

    def mine(h, zz):
        at = pl.ds(2 * zz, 2)
        return stage[h][core, at] + pair_in[h][at]

    def ring_copy(h, d, t):
        at = (d, t, d) if t == 0 else (d, t)
        return remote(rsend[h].at[at], rrecv[h].at[at], r_ss.at[h, d, t], r_rs.at[h, d, t], ring[d])

    def pass_on(h, t):
        for d in range(2):
            far = hops - t
            part = mine(h, (z + far) % nz if d == 0 else (z + nz - far) % nz)
            if t == 0:
                rsend[h][d, 0, d] = part[d].astype(BF16)
            else:
                ring_copy(h, d, t - 1).wait_recv()
                if t == 1:
                    rsend[h][d, 1, 1 - d] = part[1 - d].astype(BF16)
                    rsend[h][d, 1, d] = (part[d] + rrecv[h][d, 0, d].astype(F32)).astype(BF16)
                else:
                    rsend[h][d, t] = (part + rrecv[h][d, t - 1].astype(F32)).astype(BF16)
            ring_copy(h, d, t).start()

    def ring_end(h):
        total = mine(h, z)
        for d in range(2):
            ring_copy(h, d, hops - 1).wait_recv()
            if hops > 1:
                total = total + rrecv[h][d, hops - 1].astype(F32)
        lanes = slice(h * BS, (1 + 2 * h) * BS)
        for d in range(2):
            xsum[d, :, lanes] = total[d] if hops > 1 else total[d] + rrecv[h][d, 0, d].astype(F32)

    x_copy = remote(xsum.at[1 - xh], xrecv, x_ss, x_rs, across)

    def outer(p, begin, end):
        pad = BS - SPLIT[p][1] if p == 0 else 0

        def body(k, carry):
            halo_copy(p, 0, k).wait_recv()
            halo_copy(p, 1, k).wait_recv()
            ahead, behind = halo[p][0, k], halo[p][1, k]
            cross_a[p][0] += dot_t(e[k, rows - 2 * BS :, :], scaled(ahead, k, pad))
            cross_b[p][0] += dot_t(ahead, ss[nblk - 2, k])
            cross_a[p][1] += dot_t(e[k, : 2 * BS, :], scaled(behind, k, pad))
            cross_b[p][1] += dot_t(behind, ss[1, k])
            return carry

        lax.fori_loop(begin, end, body, 0)

    def late_pack(p):
        stored = lstage[p]
        q0, n = SPLIT[p]
        for s, gg in enumerate(a_g):
            for o in (2 * gg, 2 * gg + 1):
                for side, base in ((1, 0), (0, rows - 2 * BS)):
                    lo, hi = max(base, own * o), min(base + 2 * BS, own * (o + 1))
                    if lo >= hi:
                        continue
                    a, b = lo - own * o, hi - own * o
                    off = s * a_rows[p]
                    if p == 0:
                        part = cross_a[0][side, lo - base : hi - base]
                        stored[o % 2, off + a : off + b] = part[:, :BS]
                        stored[o % 2, off + own + a : off + own + b] = part[:, BS:]
                    else:
                        for x0, x1, lane in ((a, min(b, hr), 0), (max(a, hr), b, BS // 2)):
                            if x0 < x1:
                                from_row = lo - base - a
                                shift = off - (hr if lane else 0)
                                stored[o % 2, shift + x0 : shift + x1, lane : lane + BS // 2] = cross_a[1][
                                    side, from_row + x0 : from_row + x1
                                ]
        up, dn = b_g[p]
        todo = [(s, gg, 0, q0) for s, gg in enumerate(up)]
        todo += [(len(up) + s, gg, 1, rows - BS + q0) for s, gg in enumerate(dn)]
        for s, gg, side, base in todo:
            for o in (2 * gg, 2 * gg + 1):
                lo, hi = max(base, own * o), min(base + n, own * (o + 1))
                if lo < hi:
                    off = na * a_rows[p] + 2 * own * s
                    a, b = lo - own * o, hi - own * o
                    part = cross_b[p][side, lo - base : hi - base]
                    stored[o % 2, off + a : off + b] = part[:, :BS]
                    stored[o % 2, off + own + a : off + own + b] = part[:, BS:]

    def late_pair(p):
        return remote(lstage[p].at[1 - core], lpair_in[p], lpair_ss.at[p], lpair_rs.at[p], partner)

    def a_copy(p, s, gg, origin):
        size = a_rows[p] * (2 - p)
        return remote(
            lsend[p].at[pl.ds(s * size, size)], larecv[p].at[origin],
            la_ss.at[p, s], la_rs.at[p, origin], dev(band, 2 * gg + xh if p == 0 else gg),
        )

    def b_copy(p, s, b, gg, origin):
        size = 2 * own * (2 - p)
        return remote(
            lsend[p].at[pl.ds(na * a_rows[p] + s * size, size)], lbrecv[p].at[origin],
            lb_ss.at[p, s], lb_rs.at[p, origin], dev(b, 2 * gg + xh if p == 0 else gg),
        )

    def a_list(p):
        return list(enumerate(a_g if p else [t // 2 for t in a_g[::2]]))

    def b_list(p):
        up, dn = b_g[p] if p else [[t // 2 for t in part[::2]] for part in b_g[0]]
        return [(s, nxt, gg) for s, gg in enumerate(up)] + [
            (len(up) + s, prv, gg) for s, gg in enumerate(dn)
        ]

    def late_send(p):
        late_pair(p).wait_recv()
        lsend[p][...] = (lstage[p][core] + lpair_in[p][...]).astype(BF16)
        here = g if p else z
        for s, b, gg in b_list(p):
            b_copy(p, s, b, gg, here).start()
        for s, gg in a_list(p):
            pl.when(here != gg)(a_copy(p, s, gg, here).start)

    low = na // 2
    is_a = (g < low) | (g >= ng - low)

    def within_groups(p):
        up, dn = b_g[p]
        return ((g >= up[0]) & (g <= up[-1])) | ((g >= dn[0]) & (g <= dn[-1]))

    lx = remote(lxsum.at[:, 1 - xh], lxrecv, lx_ss, lx_rs, across)

    def late_sum0():
        @pl.when(is_a)
        def _():
            size = 4 * own
            at = pl.ds(pl.multiple_of(jnp.where(g < low, z, z - (nz - na // 2)) * size, 16), size)
            total = lstage0[core, at] + lpair0[at]
            for k in range(1, nz):
                origin = (z + k) % nz
                a_copy(0, 0, 0, origin).wait_recv()
                total = total + larecv0[origin].astype(F32)
            lxsum[0, 0] = total[: 2 * own]
            lxsum[0, 1] = total[2 * own :]

            @pl.when(within_groups(0))
            def _():
                total = jnp.zeros((4 * own, BS), F32)
                for k in range(nz):
                    b_copy(0, 0, nxt, 0, k).wait_recv()
                    total = total + lbrecv0[k].astype(F32)
                lxsum[1, 0] = total[: 2 * own]
                lxsum[1, 1] = total[2 * own :]

            lx.start()

    def late_end0():
        @pl.when(is_a)
        def _():
            lx.wait_recv()
            late_a0[...] = lxsum[0, xh] + lxrecv[0]
            late_b[...] += lxsum[1, xh] + lxrecv[1]

    def late_sum1():
        @pl.when(is_a)
        def _():
            at = pl.ds(pl.multiple_of(jnp.where(g < low, g, g - (ng - na)) * hr, 16), hr)
            total = lstage1[core, at] + lpair1[at]
            for k in range(1, ng):
                origin = (g + k) % ng
                a_copy(1, 0, 0, origin).wait_recv()
                total = total + larecv1[origin].astype(F32)
            late_a1[...] = total

        @pl.when(within_groups(1))
        def _():
            total = late_b[...]
            for k in range(ng):
                b_copy(1, 0, nxt, 0, k).wait_recv()
                total = total + lbrecv1[k].astype(F32)
            late_b[...] = total

    def cut(part):
        return nk * part // 7

    def more(begin, end):
        lax.fori_loop(cut(begin), cut(end), others, 0)

    lax.fori_loop(0, nk, diagonal, 0)
    early_pack(0)
    early_pair(0).start()
    more(0, 2)
    if hops > 1:
        relay(1)
    early_pair(0).wait_recv()
    pass_on(0, 0)
    more(2, 4)
    if hops > 2:
        relay(2)
    more(4, 6)
    for t in range(3, hops):
        relay(t)
    if hops > 1:
        pass_on(0, 1)
    more(6, 7)
    early_pack(1)
    early_pair(1).start()
    outer(0, 0, cut(2))
    if hops > 2:
        pass_on(0, 2)
    early_pair(1).wait_recv()
    pass_on(1, 0)
    outer(0, cut(2), cut(4))
    for t in range(3, hops):
        pass_on(0, t)
    if hops > 1:
        pass_on(1, 1)
    outer(0, cut(4), nk)
    late_pack(0)
    late_pair(0).start()
    ring_end(0)
    relay(hops)
    outer(1, 0, cut(3))
    if hops > 2:
        pass_on(1, 2)
    pl.semaphore_wait(ready.at[0], 1)
    pl.semaphore_wait(ready.at[1], 1)
    late_send(0)
    outer(1, cut(3), cut(5))
    for t in range(3, hops):
        pass_on(1, t)
    outer(1, cut(5), nk)
    late_pack(1)
    late_pair(1).start()
    late_send(1)
    ring_end(1)
    x_copy.start()
    late_sum0()
    late_sum1()
    late_end0()
    x_copy.wait_recv()
    early = xsum[xh] + xrecv[...]

    row_block = (lax.broadcasted_iota(jnp.int32, (own, BS), 0) + own * me) // BS
    n0, n1 = SPLIT[0][1], SPLIT[1][1]
    packed = late_a1[...]
    tail = jnp.concatenate([packed[:, : BS // 2], packed[: own - hr, BS // 2 :]], axis=0)
    for out, start, lane in ((dens, 0, 0), (edens, own, n1)):
        rows_here = slice(start, start + own)
        parts = (
            jnp.concatenate([late_a0[rows_here, :n0], tail[:, lane : lane + n1]], axis=1),
            late_b[rows_here],
        )
        for j in range(3):
            value = early[rows_here, j * BS : (j + 1) * BS]
            if j:
                for part, wanted in (
                    (parts[0], ((0, -1), (1, -1), (nblk - 2, nblk), (nblk - 1, nblk))),
                    (parts[1], ((0, -2), (nblk - 1, nblk + 1))),
                ):
                    mask = None
                    for i, rel in wanted:
                        hit = jnp.where(block_cols[j, i] - first_block == rel, i, -1)
                        mask = (row_block == hit) if mask is None else mask | (row_block == hit)
                    value = value + jnp.where(mask, part, 0.0)
            out[:, j * BS : (j + 1) * BS] = value

    for h in range(2):
        early_pair(h).wait_send()
        for t in range(hops):
            for d in range(2):
                ring_copy(h, d, t).wait_send()
    x_copy.wait_send()
    for p in range(2):
        for k in range(nk):
            halo_copy(p, 0, k).wait_send()
            halo_copy(p, 1, k).wait_send()
        late_pair(p).wait_send()
        here = g if p else z
        for s, b, gg in b_list(p):
            b_copy(p, s, b, gg, here).wait_send()
        for s, gg in a_list(p):
            pl.when(here != gg)(a_copy(p, s, gg, here).wait_send)
    pl.when(is_a)(lx.wait_send)


def packed_rows(own):
    return -(-own // 32) * 16


def outer_groups(rows, nz):
    low = -(-2 * BS // (rows // (2 * nz)))
    return list(range(low)) + list(range(2 * nz - low, 2 * nz))


def boundary_groups(rows, nz, p):
    per = rows // (2 * nz)
    q0, n = SPLIT[p]
    last = rows - BS + q0
    up, dn = (q0 // per, -(-(q0 + n) // per)), (last // per, -(-(last + n) // per))
    if p == 0:
        up, dn = ((a // 2 * 2, -(-b // 2) * 2) for a, b in (up, dn))
    return list(range(*up)), list(range(*dn))


def shards(nband, nz, cols_per_slice, chunk, eigvecs, energies, smearing, counts, occupied, block_cols):
    rows, cols = eigvecs.shape
    nk = cols // chunk
    nblk = rows // BS
    own = rows // (nz * 4)
    ng = 2 * nz
    hr = packed_rows(own)
    na = len(outer_groups(rows, nz))
    nb = [len(up) + len(dn) for up, dn in (boundary_groups(rows, nz, p) for p in range(2))]
    late0 = (na + nb[0]) * 2 * own
    late1 = na * hr + nb[1] * 2 * own
    n0, n1 = SPLIT[0][1], SPLIT[1][1]
    vmem = pl.BlockSpec(memory_space=pltpu.VMEM)
    dma = pltpu.SemaphoreType.DMA
    wide = 3 * BS
    return pl.pallas_call(
        functools.partial(kernel, nband, nz, cols_per_slice, chunk),
        out_shape=(jax.ShapeDtypeStruct((own, wide), F32),) * 2,
        in_specs=[pl.BlockSpec(memory_space=pl.ANY)] * 6,
        out_specs=(vmem, vmem),
        scratch_shapes=[
            pltpu.VMEM((cols,), F32),
            pltpu.VMEM((cols,), F32),
            pltpu.SMEM(counts.shape, jnp.int32),
            pltpu.SMEM(occupied.shape, jnp.int32),
            pltpu.SMEM((3, nblk), jnp.int32),
            pltpu.VMEM((nk, rows, chunk), BF16),
            pltpu.VMEM((1, cols), F32),
            pltpu.VMEM((1, cols), F32),
            pltpu.VMEM((nblk, nk, 2 * BS, chunk), BF16),
            pltpu.VMEM((nblk * 5, BS, 2 * BS), F32),
            pltpu.VMEM((2, nk, n0, chunk), BF16),
            pltpu.VMEM((2, nk, n1, chunk), BF16),
            pltpu.VMEM((2, 2 * BS, 2 * BS), F32),
            pltpu.VMEM((2, 2 * BS, 2 * n1), F32),
            pltpu.VMEM((2, n0, 2 * BS), F32),
            pltpu.VMEM((2, n1, 2 * BS), F32),
            pltpu.VMEM((2, ng, 2 * own, BS), F32),
            pltpu.VMEM((2, ng, 2 * own, 2 * BS), F32),
            pltpu.VMEM((ng, 2 * own, BS), F32),
            pltpu.VMEM((ng, 2 * own, 2 * BS), F32),
            pltpu.VMEM((2, nz // 2, 2, 2 * own, BS), BF16),
            pltpu.VMEM((2, nz // 2, 2, 2 * own, 2 * BS), BF16),
            pltpu.VMEM((2, nz // 2, 2, 2 * own, BS), BF16),
            pltpu.VMEM((2, nz // 2, 2, 2 * own, 2 * BS), BF16),
            pltpu.VMEM((2, 2 * own, wide), F32),
            pltpu.VMEM((2 * own, wide), F32),
            pltpu.VMEM((2, late0, BS), F32),
            pltpu.VMEM((2, late1, BS), F32),
            pltpu.VMEM((late0, BS), F32),
            pltpu.VMEM((late1, BS), F32),
            pltpu.VMEM((late0, BS), BF16),
            pltpu.VMEM((late1, BS), BF16),
            pltpu.VMEM((nz, 4 * own, BS), BF16),
            pltpu.VMEM((ng, hr, BS), BF16),
            pltpu.VMEM((nz, 4 * own, BS), BF16),
            pltpu.VMEM((ng, 2 * own, BS), BF16),
            pltpu.VMEM((2, 2, 2 * own, BS), F32),
            pltpu.VMEM((2, 2 * own, BS), F32),
            pltpu.VMEM((2 * own, BS), F32),
            pltpu.VMEM((hr, BS), F32),
            pltpu.VMEM((2 * own, BS), F32),
            pltpu.SemaphoreType.REGULAR((2, nz // 2)), pltpu.SemaphoreType.REGULAR((2,)),
            dma((5,)), dma((nk,)), dma((2, 2, nk)), dma((2, 2, nk)), dma((2,)), dma((2,)),
            dma((2, 2, nz // 2)), dma((2, 2, nz // 2)), dma, dma,
            dma((2,)), dma((2,)), dma((2, na)), dma((2, ng)), dma((2, max(nb))), dma((2, ng)), dma, dma,
        ],
        compiler_params=pltpu.CompilerParams(
            collective_id=0, has_side_effects=True, vmem_limit_bytes=VMEM_LIMIT
        ),
        cost_estimate=pl.CostEstimate(
            flops=2 * 48 * BS * BS * cols, bytes_accessed=rows * cols * 2, transcendentals=0
        ),
    )(eigvecs, energies, smearing, counts, occupied, block_cols.T)


def build(mesh, cols_per_slice, chunk):
    placed = (P("band", "cuts"), P("cuts"), P("cuts"), P("cuts"), P("cuts"), P("band", None))
    body = functools.partial(shards, mesh.shape["band"], mesh.shape["cuts"] // 4, cols_per_slice, chunk)
    return jax.shard_map(
        body,
        mesh=mesh,
        in_specs=placed,
        out_specs=(P(("band", "cuts"), None), P(("band", "cuts"), None)),
        check_vma=False,
    )


def solution(mesh):
    return build(mesh, COLS, CHUNK)
```

```python
import functools

import jax
import jax.numpy as jnp
from jax import lax
from jax.experimental import pallas as pl
from jax.experimental.pallas import tpu as pltpu
from jax.sharding import PartitionSpec as P

BS = 128
COLS = 1792
CHUNK = 896
SPLIT = ((0, 96), (96, 32))
VMEM_LIMIT = 60 * 1024 * 1024
MESH = pl.DeviceIdType.MESH
F32, BF16 = jnp.float32, jnp.bfloat16


def dot_t(a, b):
    return lax.dot_general(a, b, (((1,), (1,)), ((), ())), preferred_element_type=F32)


def kernel(
    nband, nz, cols_per_slice, chunk,
    eig, energies_in, smearing_in, counts_in, occupied_in, cols_in, dens, edens,
    energies, smearing, counts, occupied, block_cols, e, w, we, ss, q,
    halo0, halo1, cross_a0, cross_a1, cross_b0, cross_b1,
    stage0, stage1, pair0, pair1, rsend0, rsend1, rrecv0, rrecv1, xsum, xrecv,
    lstage0, lstage1, lpair0, lpair1, lsend0, lsend1, larecv0, larecv1, lbrecv0, lbrecv1,
    lxsum, lxrecv, late_a0, late_a1, late_b,
    wave, ready, small_sem, load_sem, halo_ss, halo_rs, pair_ss, pair_rs, r_ss, r_rs, x_ss, x_rs,
    lpair_ss, lpair_rs, la_ss, la_rs, lb_ss, lb_rs, lx_ss, lx_rs,
):
    rows, cols = eig.shape
    nk = cols // chunk
    nblk = rows // BS
    own = dens.shape[0]
    hr = packed_rows(own)
    ng = 2 * nz
    halo, cross_a, cross_b = (halo0, halo1), (cross_a0, cross_a1), (cross_b0, cross_b1)
    lstage, lpair_in, lsend = (lstage0, lstage1), (lpair0, lpair1), (lsend0, lsend1)
    larecv, lbrecv = (larecv0, larecv1), (lbrecv0, lbrecv1)
    stage, pair_in, rsend, rrecv = (stage0, stage1), (pair0, pair1), (rsend0, rsend1), (rrecv0, rrecv1)
    a_rows = (2 * own, hr)
    a_g = outer_groups(rows, nz)
    na = len(a_g)
    b_g = [boundary_groups(rows, nz, p) for p in range(2)]

    me = lax.axis_index("cuts")
    band = lax.axis_index("band")
    g, core = me // 2, me % 2
    z, xh = g // 2, g % 2
    nxt, prv = (band + 1) % nband, (band + nband - 1) % nband

    def dev(b, gg):
        return {"cuts": gg * 2 + core, "band": b}

    across = {"cuts": z * 4 + (1 - xh) * 2 + core, "band": band}
    partner = {"cuts": g * 2 + 1 - core, "band": band}

    def remote(src, dst, send_sem, recv_sem, device):
        return pltpu.make_async_remote_copy(
            src_ref=src, dst_ref=dst, send_sem=send_sem, recv_sem=recv_sem,
            device_id=device, device_id_type=MESH,
        )

    barrier = pltpu.get_barrier_semaphore()

    def greet(device):
        pl.semaphore_signal(barrier, inc=1, device_id=device, device_id_type=MESH)

    greet(dev(nxt, g))
    greet(dev(prv, g))
    ring = (dev(band, (z + 1) % nz * 2 + xh), dev(band, (z + nz - 1) % nz * 2 + xh))
    greet(ring[0])
    greet(ring[1])
    greet(across)
    greet(partner)

    smalls = []
    for t, (src, dst) in enumerate((
        (energies_in, energies), (smearing_in, smearing),
        (counts_in, counts), (occupied_in, occupied), (cols_in, block_cols),
    )):
        small = pltpu.make_async_copy(src, dst, small_sem.at[t])
        small.start()
        smalls.append(small)
    for k in range(nk):
        pltpu.make_async_copy(eig.at[:, pl.ds(k * chunk, chunk)], e.at[k], load_sem.at[k]).start()

    pl.semaphore_wait(barrier, 6)

    def halo_copy(p, side, k):
        q0, n = SPLIT[p]
        first = q0 if side == 0 else rows - BS + q0
        start = k * chunk if isinstance(k, int) else pl.multiple_of(k * chunk, 128)
        return remote(
            eig.at[pl.ds(first, n), pl.ds(start, chunk)], halo[p].at[side, k],
            halo_ss.at[p, side, k], halo_rs.at[p, side, k], dev(prv if side == 0 else nxt, g),
        )

    for p in range(2):
        for k in range(nk):
            halo_copy(p, 0, k).start()
            halo_copy(p, 1, k).start()

    def tell(sem, device):
        pl.semaphore_signal(sem, inc=1, device_id=device, device_id_type=MESH)

    def relay(t):
        for d in range(2):
            if t:
                pl.semaphore_wait(wave.at[d, t - 1], 1)
            if t < nz // 2:
                tell(wave.at[d, t], ring[d])
            elif d == 1:
                tell(ready.at[0], dev(nxt, g))
                tell(ready.at[1], dev(prv, g))

    relay(0)
    for small in smalls:
        small.wait()
    slot = lax.broadcasted_iota(jnp.int32, (1, cols), 1)
    weight = jnp.zeros((1, cols), F32)
    for s in range(cols // cols_per_slice):
        within = slot - s * cols_per_slice
        live = (within >= 0) & (within < counts[s])
        weight = jnp.where(live, jnp.where(within < occupied[s], 2.0, smearing[...].reshape(1, cols)), weight)
    w[...] = weight
    we[...] = weight * energies[...].reshape(1, cols)

    def scaled(block, k, pad=0):
        at = pl.ds(pl.multiple_of(k * chunk, 128), chunk)
        wide = block.astype(F32)
        parts = [(wide * w[:, at]).astype(BF16), (wide * we[:, at]).astype(BF16)]
        if pad:
            gap = jnp.zeros((pad, chunk), BF16)
            parts = [parts[0], gap, parts[1], gap]
        return jnp.concatenate(parts, axis=0)

    for ref in (q, cross_a0, cross_a1, cross_b0, cross_b1, lstage0, lstage1, lxsum, late_a0, late_a1, late_b):
        ref[...] = jnp.zeros_like(ref)

    def diagonal(k, carry):
        pltpu.make_async_copy(
            eig.at[:, pl.ds(pl.multiple_of(k * chunk, 128), chunk)], e.at[k], load_sem.at[k]
        ).wait()
        for j in range(nblk):
            block = e[k, j * BS : (j + 1) * BS, :]
            both = scaled(block, k)
            ss[j, k] = both
            q[j * 5 + 2] += dot_t(block, both)
        return carry

    def others(k, carry):
        for j in range(nblk):
            near = [i for i in range(max(j - 2, 0), min(j + 3, nblk)) if i != j]
            left = jnp.concatenate([e[k, i * BS : (i + 1) * BS, :] for i in near], axis=0)
            got = dot_t(left, ss[j, k])
            for t, i in enumerate(near):
                q[i * 5 + j - i + 2] += got[t * BS : (t + 1) * BS]
        return carry

    first_block = band * nblk

    def early_pack(h):
        for i in range(nblk):
            for j in ((0,), (1, 2))[h]:
                d = 2 if j == 0 else jnp.clip(block_cols[j, i] - first_block - i + 2, 0, 4)
                block = q[i * 5 + d]
                lanes = slice((j - h) * BS, (j - h + 1) * BS)
                for o in range(i * BS // own, -(-(i + 1) * BS // own)):
                    lo, hi = max(i * BS, own * o), min((i + 1) * BS, own * (o + 1))
                    part = block[lo - i * BS : hi - i * BS]
                    at = (o % 2, o // 2)
                    stage[h][at + (slice(lo - own * o, hi - own * o), lanes)] = part[:, :BS]
                    stage[h][at + (slice(own + lo - own * o, own + hi - own * o), lanes)] = part[:, BS:]

    def early_pair(h):
        return remote(stage[h].at[1 - core], pair_in[h], pair_ss.at[h], pair_rs.at[h], partner)

    hops = nz // 2

    def mine(h, zz):
        at = pl.ds(2 * zz, 2)
        return stage[h][core, at] + pair_in[h][at]

    def ring_copy(h, d, t):
        at = (d, t, d) if t == 0 else (d, t)
        return remote(rsend[h].at[at], rrecv[h].at[at], r_ss.at[h, d, t], r_rs.at[h, d, t], ring[d])

    def pass_on(h, t):
        for d in range(2):
            far = hops - t
            part = mine(h, (z + far) % nz if d == 0 else (z + nz - far) % nz)
            if t == 0:
                rsend[h][d, 0, d] = part[d].astype(BF16)
            else:
                ring_copy(h, d, t - 1).wait_recv()
                if t == 1:
                    rsend[h][d, 1, 1 - d] = part[1 - d].astype(BF16)
                    rsend[h][d, 1, d] = (part[d] + rrecv[h][d, 0, d].astype(F32)).astype(BF16)
                else:
                    rsend[h][d, t] = (part + rrecv[h][d, t - 1].astype(F32)).astype(BF16)
            ring_copy(h, d, t).start()

    def ring_end(h):
        total = mine(h, z)
        for d in range(2):
            ring_copy(h, d, hops - 1).wait_recv()
            if hops > 1:
                total = total + rrecv[h][d, hops - 1].astype(F32)
        lanes = slice(h * BS, (1 + 2 * h) * BS)
        for d in range(2):
            xsum[d, :, lanes] = total[d] if hops > 1 else total[d] + rrecv[h][d, 0, d].astype(F32)

    x_copy = remote(xsum.at[1 - xh], xrecv, x_ss, x_rs, across)

    def outer(p, begin, end):
        pad = BS - SPLIT[p][1] if p == 0 else 0

        def body(k, carry):
            halo_copy(p, 0, k).wait_recv()
            halo_copy(p, 1, k).wait_recv()
            ahead, behind = halo[p][0, k], halo[p][1, k]
            cross_a[p][0] += dot_t(e[k, rows - 2 * BS :, :], scaled(ahead, k, pad))
            cross_b[p][0] += dot_t(ahead, ss[nblk - 2, k])
            cross_a[p][1] += dot_t(e[k, : 2 * BS, :], scaled(behind, k, pad))
            cross_b[p][1] += dot_t(behind, ss[1, k])
            return carry

        lax.fori_loop(begin, end, body, 0)

    def late_pack(p):
        stored = lstage[p]
        q0, n = SPLIT[p]
        for s, gg in enumerate(a_g):
            for o in (2 * gg, 2 * gg + 1):
                for side, base in ((1, 0), (0, rows - 2 * BS)):
                    lo, hi = max(base, own * o), min(base + 2 * BS, own * (o + 1))
                    if lo >= hi:
                        continue
                    a, b = lo - own * o, hi - own * o
                    off = s * a_rows[p]
                    if p == 0:
                        part = cross_a[0][side, lo - base : hi - base]
                        stored[o % 2, off + a : off + b] = part[:, :BS]
                        stored[o % 2, off + own + a : off + own + b] = part[:, BS:]
                    else:
                        for x0, x1, lane in ((a, min(b, hr), 0), (max(a, hr), b, BS // 2)):
                            if x0 < x1:
                                from_row = lo - base - a
                                shift = off - (hr if lane else 0)
                                stored[o % 2, shift + x0 : shift + x1, lane : lane + BS // 2] = cross_a[1][
                                    side, from_row + x0 : from_row + x1
                                ]
        up, dn = b_g[p]
        todo = [(s, gg, 0, q0) for s, gg in enumerate(up)]
        todo += [(len(up) + s, gg, 1, rows - BS + q0) for s, gg in enumerate(dn)]
        for s, gg, side, base in todo:
            for o in (2 * gg, 2 * gg + 1):
                lo, hi = max(base, own * o), min(base + n, own * (o + 1))
                if lo < hi:
                    off = na * a_rows[p] + 2 * own * s
                    a, b = lo - own * o, hi - own * o
                    part = cross_b[p][side, lo - base : hi - base]
                    stored[o % 2, off + a : off + b] = part[:, :BS]
                    stored[o % 2, off + own + a : off + own + b] = part[:, BS:]

    def late_pair(p):
        return remote(lstage[p].at[1 - core], lpair_in[p], lpair_ss.at[p], lpair_rs.at[p], partner)

    def a_copy(p, s, gg, origin):
        size = a_rows[p] * (2 - p)
        return remote(
            lsend[p].at[pl.ds(s * size, size)], larecv[p].at[origin],
            la_ss.at[p, s], la_rs.at[p, origin], dev(band, 2 * gg + xh if p == 0 else gg),
        )

    def b_copy(p, s, b, gg, origin):
        size = 2 * own * (2 - p)
        return remote(
            lsend[p].at[pl.ds(na * a_rows[p] + s * size, size)], lbrecv[p].at[origin],
            lb_ss.at[p, s], lb_rs.at[p, origin], dev(b, 2 * gg + xh if p == 0 else gg),
        )

    def a_list(p):
        return list(enumerate(a_g if p else [t // 2 for t in a_g[::2]]))

    def b_list(p):
        up, dn = b_g[p] if p else [[t // 2 for t in part[::2]] for part in b_g[0]]
        return [(s, nxt, gg) for s, gg in enumerate(up)] + [
            (len(up) + s, prv, gg) for s, gg in enumerate(dn)
        ]

    def late_send(p):
        late_pair(p).wait_recv()
        lsend[p][...] = (lstage[p][core] + lpair_in[p][...]).astype(BF16)
        here = g if p else z
        for s, b, gg in b_list(p):
            b_copy(p, s, b, gg, here).start()
        for s, gg in a_list(p):
            pl.when(here != gg)(a_copy(p, s, gg, here).start)

    low = na // 2
    is_a = (g < low) | (g >= ng - low)

    def within_groups(p):
        up, dn = b_g[p]
        return ((g >= up[0]) & (g <= up[-1])) | ((g >= dn[0]) & (g <= dn[-1]))

    lx = remote(lxsum.at[:, 1 - xh], lxrecv, lx_ss, lx_rs, across)

    def late_sum0():
        @pl.when(is_a)
        def _():
            size = 4 * own
            at = pl.ds(pl.multiple_of(jnp.where(g < low, z, z - (nz - na // 2)) * size, 16), size)
            total = lstage0[core, at] + lpair0[at]
            for k in range(1, nz):
                origin = (z + k) % nz
                a_copy(0, 0, 0, origin).wait_recv()
                total = total + larecv0[origin].astype(F32)
            lxsum[0, 0] = total[: 2 * own]
            lxsum[0, 1] = total[2 * own :]

            @pl.when(within_groups(0))
            def _():
                total = jnp.zeros((4 * own, BS), F32)
                for k in range(nz):
                    b_copy(0, 0, nxt, 0, k).wait_recv()
                    total = total + lbrecv0[k].astype(F32)
                lxsum[1, 0] = total[: 2 * own]
                lxsum[1, 1] = total[2 * own :]

            lx.start()

    def late_end0():
        @pl.when(is_a)
        def _():
            lx.wait_recv()
            late_a0[...] = lxsum[0, xh] + lxrecv[0]
            late_b[...] += lxsum[1, xh] + lxrecv[1]

    def late_sum1():
        @pl.when(is_a)
        def _():
            at = pl.ds(pl.multiple_of(jnp.where(g < low, g, g - (ng - na)) * hr, 16), hr)
            total = lstage1[core, at] + lpair1[at]
            for k in range(1, ng):
                origin = (g + k) % ng
                a_copy(1, 0, 0, origin).wait_recv()
                total = total + larecv1[origin].astype(F32)
            late_a1[...] = total

        @pl.when(within_groups(1))
        def _():
            total = late_b[...]
            for k in range(ng):
                b_copy(1, 0, nxt, 0, k).wait_recv()
                total = total + lbrecv1[k].astype(F32)
            late_b[...] = total

    def cut(part):
        return nk * part // 7

    def more(begin, end):
        lax.fori_loop(cut(begin), cut(end), others, 0)

    lax.fori_loop(0, nk, diagonal, 0)
    early_pack(0)
    early_pair(0).start()
    more(0, 2)
    if hops > 1:
        relay(1)
    early_pair(0).wait_recv()
    pass_on(0, 0)
    more(2, 4)
    if hops > 2:
        relay(2)
    more(4, 6)
    for t in range(3, hops):
        relay(t)
    if hops > 1:
        pass_on(0, 1)
    more(6, 7)
    early_pack(1)
    early_pair(1).start()
    outer(0, 0, cut(2))
    if hops > 2:
        pass_on(0, 2)
    early_pair(1).wait_recv()
    pass_on(1, 0)
    outer(0, cut(2), cut(4))
    for t in range(3, hops):
        pass_on(0, t)
    if hops > 1:
        pass_on(1, 1)
    outer(0, cut(4), nk)
    late_pack(0)
    late_pair(0).start()
    ring_end(0)
    relay(hops)
    outer(1, 0, cut(3))
    if hops > 2:
        pass_on(1, 2)
    pl.semaphore_wait(ready.at[0], 1)
    pl.semaphore_wait(ready.at[1], 1)
    late_send(0)
    outer(1, cut(3), cut(5))
    for t in range(3, hops):
        pass_on(1, t)
    outer(1, cut(5), nk)
    late_pack(1)
    late_pair(1).start()
    late_send(1)
    ring_end(1)
    x_copy.start()
    late_sum0()
    late_sum1()
    late_end0()
    x_copy.wait_recv()
    early = xsum[xh] + xrecv[...]

    row_block = (lax.broadcasted_iota(jnp.int32, (own, BS), 0) + own * me) // BS
    n0, n1 = SPLIT[0][1], SPLIT[1][1]
    packed = late_a1[...]
    tail = jnp.concatenate([packed[:, : BS // 2], packed[: own - hr, BS // 2 :]], axis=0)
    for out, start, lane in ((dens, 0, 0), (edens, own, n1)):
        rows_here = slice(start, start + own)
        parts = (
            jnp.concatenate([late_a0[rows_here, :n0], tail[:, lane : lane + n1]], axis=1),
            late_b[rows_here],
        )
        for j in range(3):
            value = early[rows_here, j * BS : (j + 1) * BS]
            if j:
                for part, wanted in (
                    (parts[0], ((0, -1), (1, -1), (nblk - 2, nblk), (nblk - 1, nblk))),
                    (parts[1], ((0, -2), (nblk - 1, nblk + 1))),
                ):
                    mask = None
                    for i, rel in wanted:
                        hit = jnp.where(block_cols[j, i] - first_block == rel, i, -1)
                        mask = (row_block == hit) if mask is None else mask | (row_block == hit)
                    value = value + jnp.where(mask, part, 0.0)
            out[:, j * BS : (j + 1) * BS] = value

    for h in range(2):
        early_pair(h).wait_send()
        for t in range(hops):
            for d in range(2):
                ring_copy(h, d, t).wait_send()
    x_copy.wait_send()
    for p in range(2):
        for k in range(nk):
            halo_copy(p, 0, k).wait_send()
            halo_copy(p, 1, k).wait_send()
        late_pair(p).wait_send()
        here = g if p else z
        for s, b, gg in b_list(p):
            b_copy(p, s, b, gg, here).wait_send()
        for s, gg in a_list(p):
            pl.when(here != gg)(a_copy(p, s, gg, here).wait_send)
    pl.when(is_a)(lx.wait_send)


def packed_rows(own):
    return -(-own // 32) * 16


def outer_groups(rows, nz):
    low = -(-2 * BS // (rows // (2 * nz)))
    return list(range(low)) + list(range(2 * nz - low, 2 * nz))


def boundary_groups(rows, nz, p):
    per = rows // (2 * nz)
    q0, n = SPLIT[p]
    last = rows - BS + q0
    up, dn = (q0 // per, -(-(q0 + n) // per)), (last // per, -(-(last + n) // per))
    if p == 0:
        up, dn = ((a // 2 * 2, -(-b // 2) * 2) for a, b in (up, dn))
    return list(range(*up)), list(range(*dn))


def shards(nband, nz, cols_per_slice, chunk, eigvecs, energies, smearing, counts, occupied, block_cols):
    rows, cols = eigvecs.shape
    nk = cols // chunk
    nblk = rows // BS
    own = rows // (nz * 4)
    ng = 2 * nz
    hr = packed_rows(own)
    na = len(outer_groups(rows, nz))
    nb = [len(up) + len(dn) for up, dn in (boundary_groups(rows, nz, p) for p in range(2))]
    late0 = (na + nb[0]) * 2 * own
    late1 = na * hr + nb[1] * 2 * own
    n0, n1 = SPLIT[0][1], SPLIT[1][1]
    vmem = pl.BlockSpec(memory_space=pltpu.VMEM)
    dma = pltpu.SemaphoreType.DMA
    wide = 3 * BS
    return pl.pallas_call(
        functools.partial(kernel, nband, nz, cols_per_slice, chunk),
        out_shape=(jax.ShapeDtypeStruct((own, wide), F32),) * 2,
        in_specs=[pl.BlockSpec(memory_space=pl.ANY)] * 6,
        out_specs=(vmem, vmem),
        scratch_shapes=[
            pltpu.VMEM((cols,), F32),
            pltpu.VMEM((cols,), F32),
            pltpu.SMEM(counts.shape, jnp.int32),
            pltpu.SMEM(occupied.shape, jnp.int32),
            pltpu.SMEM((3, nblk), jnp.int32),
            pltpu.VMEM((nk, rows, chunk), BF16),
            pltpu.VMEM((1, cols), F32),
            pltpu.VMEM((1, cols), F32),
            pltpu.VMEM((nblk, nk, 2 * BS, chunk), BF16),
            pltpu.VMEM((nblk * 5, BS, 2 * BS), F32),
            pltpu.VMEM((2, nk, n0, chunk), BF16),
            pltpu.VMEM((2, nk, n1, chunk), BF16),
            pltpu.VMEM((2, 2 * BS, 2 * BS), F32),
            pltpu.VMEM((2, 2 * BS, 2 * n1), F32),
            pltpu.VMEM((2, n0, 2 * BS), F32),
            pltpu.VMEM((2, n1, 2 * BS), F32),
            pltpu.VMEM((2, ng, 2 * own, BS), F32),
            pltpu.VMEM((2, ng, 2 * own, 2 * BS), F32),
            pltpu.VMEM((ng, 2 * own, BS), F32),
            pltpu.VMEM((ng, 2 * own, 2 * BS), F32),
            pltpu.VMEM((2, nz // 2, 2, 2 * own, BS), BF16),
            pltpu.VMEM((2, nz // 2, 2, 2 * own, 2 * BS), BF16),
            pltpu.VMEM((2, nz // 2, 2, 2 * own, BS), BF16),
            pltpu.VMEM((2, nz // 2, 2, 2 * own, 2 * BS), BF16),
            pltpu.VMEM((2, 2 * own, wide), F32),
            pltpu.VMEM((2 * own, wide), F32),
            pltpu.VMEM((2, late0, BS), F32),
            pltpu.VMEM((2, late1, BS), F32),
            pltpu.VMEM((late0, BS), F32),
            pltpu.VMEM((late1, BS), F32),
            pltpu.VMEM((late0, BS), BF16),
            pltpu.VMEM((late1, BS), BF16),
            pltpu.VMEM((nz, 4 * own, BS), BF16),
            pltpu.VMEM((ng, hr, BS), BF16),
            pltpu.VMEM((nz, 4 * own, BS), BF16),
            pltpu.VMEM((ng, 2 * own, BS), BF16),
            pltpu.VMEM((2, 2, 2 * own, BS), F32),
            pltpu.VMEM((2, 2 * own, BS), F32),
            pltpu.VMEM((2 * own, BS), F32),
            pltpu.VMEM((hr, BS), F32),
            pltpu.VMEM((2 * own, BS), F32),
            pltpu.SemaphoreType.REGULAR((2, nz // 2)), pltpu.SemaphoreType.REGULAR((2,)),
            dma((5,)), dma((nk,)), dma((2, 2, nk)), dma((2, 2, nk)), dma((2,)), dma((2,)),
            dma((2, 2, nz // 2)), dma((2, 2, nz // 2)), dma, dma,
            dma((2,)), dma((2,)), dma((2, na)), dma((2, ng)), dma((2, max(nb))), dma((2, ng)), dma, dma,
        ],
        compiler_params=pltpu.CompilerParams(
            collective_id=0, has_side_effects=True, vmem_limit_bytes=VMEM_LIMIT
        ),
        cost_estimate=pl.CostEstimate(
            flops=2 * 48 * BS * BS * cols, bytes_accessed=rows * cols * 2, transcendentals=0
        ),
    )(eigvecs, energies, smearing, counts, occupied, block_cols.T)


def build(mesh, cols_per_slice, chunk):
    placed = (P("band", "cuts"), P("cuts"), P("cuts"), P("cuts"), P("cuts"), P("band", None))
    body = functools.partial(shards, mesh.shape["band"], mesh.shape["cuts"] // 4, cols_per_slice, chunk)
    return jax.shard_map(
        body,
        mesh=mesh,
        in_specs=placed,
        out_specs=(P(("band", "cuts"), None), P(("band", "cuts"), None)),
        check_vma=False,
    )


def solution(mesh):
    return build(mesh, COLS, CHUNK)
```
